128 devices in a mesh: dp: 4 (over x), grid: 32 (over y, z, core).
Axes of the slice: x: 4, y: 4, z: 4, core: 2. Of those that a mesh axis runs over, the one named last changes fastest.
Arguments:
- embeddings: bfloat16 [40960, 768], P(('dp', 'grid')), may hold values from -6 to 6
- cluster: int32 [40960, 1], P(('dp', 'grid')), may hold values from 0 to 3; in each aligned block of 320 rows (0 to 319, 320 to 639, ...) at most 160 rows name the same one
- order_key: int32 [40960], P(('dp', 'grid')), may hold values from 0 to 40959, each once
Outputs:
- best: float32 [40960], P(('dp', 'grid'))
The draws below stay inside these ranges and needn't reach their ends.
Inputs may be any that keep to these rules, and one draw needn't show every extreme that they name: In the rows of one device at most 160 rows name one cluster, and on some device one cluster is named by exactly 160 rows; every cluster is named. `order_key`: each number of 0 to 40959 appears once.
All inputs are finite; a program needn't handle non-finite values.
Results may differ from the reference program's by a relative error of at most 0.0012.
Values may be sent and summed in bfloat16 or wider, within the bound.
A program may use at most 128 MiB of HBM per device.

```python
import math
import jax
import jax.numpy as jnp
import numpy as np
from jax import lax

E = 768
R_DEV = 320
MOST = 160
CLUSTERS = 4
ROWS = 40960


def shard_levels(own_key, dims, cuts, smallest, high):
    def one(axis_at, shards_of):
        draws = jax.random.uniform(jax.random.fold_in(jax.random.fold_in(own_key, 6), axis_at), (shards_of,), jnp.float32, smallest / len(cuts), high / len(cuts))
        return jnp.repeat(jnp.exp(draws), dims[axis_at] // shards_of).reshape((-1,) + (1,) * (len(dims) - axis_at - 1))

    gain = one(*cuts[0])
    for cut in cuts[1:]:
        gain = gain * one(*cut)
    return gain


def shared_out(stream_key, own, number, rows, amount, top, most, skew):
    order = jax.random.permutation(stream_key, amount)
    packed, usual = load_shares(amount, rows * top, most, skew, True), load_shares(amount, rows * top, most, skew, False)
    places = jnp.arange(amount)

    def named(tallies, rotation):
        used = int((tallies > 0).sum())
        fixed = max(1, used // 4)
        passed = fixed + (places - fixed + rotation * (used - fixed)) % max(1, amount - fixed)
        return jnp.zeros((amount,), jnp.int32).at[order[jnp.where(places < fixed, places, passed)]].set(jnp.asarray(tallies, jnp.int32))

    tallies = jnp.where(number % 4 == 0, named(packed, number // 4), named(usual, number - number // 4 - 1))
    mixed = jax.random.permutation(jax.random.fold_in(own, 3), amount)
    donor, sink = mixed[0:amount // 2 * 2:2], mixed[1:amount // 2 * 2:2]
    slack = jnp.minimum(tallies[donor] - 1, most - tallies[sink]) // 2
    slack = jnp.where((donor == order[0]) | (sink == order[0]) | (tallies[sink] == 0), 0, jnp.maximum(slack, 0))
    passed = jax.random.randint(jax.random.fold_in(own, 4), (amount // 2,), 0, 1 << 20) % (slack + 1)
    tallies = tallies.at[donor].add(-passed).at[sink].add(passed)
    items = jnp.searchsorted(jnp.cumsum(tallies), jnp.arange(rows * top), side="right").astype(jnp.int32)
    listing = items.reshape(top, rows).T
    listing = listing[jax.random.permutation(jax.random.fold_in(own, 1), rows)]
    rotation = jax.random.randint(jax.random.fold_in(own, 2), (rows, 1), 0, top)
    return jnp.take_along_axis(listing, (jnp.arange(top)[None, :] + rotation) % top, axis=1)


def load_shares(number_of, total, most, skew, full):
    weights = [(1 << 20) // math.isqrt(grade ** skew) + 1 for grade in range(1, number_of + 1)]
    largest = most if full else min(most, max(-(-total // number_of), total * weights[0] // sum(weights)))
    least = 1 if total - largest >= number_of - 1 else 0
    given, spare = [largest] + [least] * (number_of - 1), total - largest - least * (number_of - 1)
    while spare > 0:
        candidates = [i for i in range(1, number_of) if given[i] < largest] or [i for i in range(1, number_of) if given[i] < most]
        mass, remaining = sum([weights[i] for i in candidates]), spare
        for i in candidates:
            addition = min(most - given[i], max(1, remaining * weights[i] // mass), spare)
            given[i] = given[i] + addition
            spare = spare - addition
    return np.array(given)


def bell_draw(stream_key, dims, spread, reach, shards=(), kind=jnp.bfloat16):
    values = jax.random.normal(stream_key, dims, jnp.float32) * spread
    if len(shards) > 0:
        values = shard_levels(stream_key, dims, shards, -0.22, 0.18) * values
    return jnp.clip(values, min=-reach, max=reach).astype(kind)


def setup_inputs(seed: int = 0) -> dict:
    streams_of = jax.random.split(jax.random.key(seed), 4)
    embeddings = bell_draw(streams_of[0], (ROWS, E), 1.0, 6.0, ((0, 128),))
    cluster_keys = jax.random.split(jax.random.fold_in(streams_of[1], 1), ROWS // R_DEV)
    cluster_turns = jax.random.permutation(jax.random.fold_in(streams_of[1], 3), ROWS // R_DEV)
    cluster = jax.vmap(lambda own, number: shared_out(jax.random.fold_in(streams_of[1], 2), own, number, R_DEV, CLUSTERS, 1, MOST, 1))(cluster_keys, cluster_turns).reshape((ROWS, 1))
    order_key = jax.random.permutation(streams_of[2], ROWS).astype(jnp.int32)
    return {"embeddings": embeddings, "cluster": cluster, "order_key": order_key}


def reference(embeddings, cluster, order_key):
    values = embeddings.astype(jnp.float32)
    scaled = values * lax.rsqrt(lax.optimization_barrier(jnp.sum(values * values, axis=1, keepdims=True)) + 1e-06)
    units = lax.optimization_barrier(scaled.astype(jnp.bfloat16)).astype(jnp.float32)
    labels = cluster[:, 0]
    blocks = units.shape[0] // R_DEV

    def one_block(index):
        start = (index * R_DEV).astype(jnp.int32)
        queries = lax.dynamic_slice_in_dim(units, start, R_DEV, 0)
        query_labels = lax.dynamic_slice_in_dim(labels, start, R_DEV, 0)
        query_keys = lax.dynamic_slice_in_dim(order_key, start, R_DEV, 0)
        sims = jnp.dot(queries, units.T, precision=lax.Precision.HIGHEST, preferred_element_type=jnp.float32)
        allowed = (labels[None, :] == query_labels[:, None]) & (order_key[None, :] < query_keys[:, None])
        return lax.optimization_barrier(jnp.max(jnp.where(allowed, sims, jnp.float32(-1.0)), axis=1))
    return lax.map(one_block, jnp.arange(blocks, dtype=jnp.int32)).reshape(-1)
```

```python
import functools

import jax
import jax.numpy as jnp
from jax import lax
from jax.experimental import pallas as pl
from jax.experimental.pallas import tpu as pltpu
from jax.sharding import PartitionSpec as P

MESH = pl.DeviceIdType.MESH
NT = (((1,), (1,)), ((), ()))
epsilon = 1e-06
scale = 65536.0

OFFSETS = {
    "o": (0, 0, 0), "a": (0, 0, 1), "b": (0, 0, 2), "c": (0, 1, 0), "d": (0, 1, 2), "e": (0, 1, 3),
    "f": (0, 3, 0), "g": (1, 0, 0), "h": (2, 0, 0), "i": (2, 3, 0), "j": (3, 1, 3), "k": (3, 3, 0),
}
FULL = "oacfgkebhd"
HALF = "ij"
BLOCKS = FULL + HALF
SLOT = {b: n for n, b in enumerate(BLOCKS)}
CHUNKS = 5
ONE_WAY = {"oo", "cf", "df", "dc", "di", "bh", "ho", "ic", "id"}
COLUMNS = "acgfekdbh"
RETURNED = "acgfekdbhij"


def kernel(rows, width, x_ref, meta_in, out_ref, full, half, meta, col_c, col_g, acc_row, acc_col, ret, back,
           send, recv, d2d_send, d2d_recv, m_send, m_recv, md_send, md_recv, r_send, r_recv):
    x, grid = lax.axis_index("dp"), lax.axis_index("grid")
    y, z, core = grid // 8, (grid // 2) % 4, grid % 2
    pair_rows = 2 * rows
    step = rows // CHUNKS
    mine = pl.multiple_of(core * rows, step)

    def device(offset, which):
        dx, dy, dz = offset
        return ((x + dx) % 4, ((y + dy) % 4) * 8 + ((z + dz) % 4) * 2 + which)

    def minus(offset):
        return tuple(-v for v in offset)

    sibling = device((0, 0, 0), 1 - core)
    barrier = pltpu.get_barrier_semaphore()
    partners = {((0, 0, 0), 1)}
    for b in BLOCKS[1:]:
        for offset in (OFFSETS[b], tuple(-v % 4 for v in OFFSETS[b])):
            partners.add((offset, 0))
            if b in FULL:
                partners.add((offset, 1))
    neighbours = [device(offset, 1 - core if other else core) for offset, other in sorted(partners)]
    for n in neighbours:
        pl.semaphore_signal(barrier, inc=1, device_id=n, device_id_type=MESH)

    def place(b, s):
        if b in FULL:
            return full.at[SLOT[b], pl.ds(pl.multiple_of(core * rows + s * step, step), step)]
        return half.at[SLOT[b] - len(FULL), pl.ds(s * step, step)]

    pending = []

    def hop(source, target, s):
        offset = tuple((q - p) % 4 for p, q in zip(OFFSETS[source], OFFSETS[target]))
        c = pltpu.make_async_remote_copy(
            src_ref=place(source, s), dst_ref=place(target, s),
            send_sem=send.at[SLOT[target], s], recv_sem=recv.at[SLOT[target], s],
            device_id=device(offset, core), device_id_type=MESH)
        c.start()
        pending.append(c)

    def got(b, s):
        here = place(b, s)
        pltpu.make_async_copy(here, here, recv.at[SLOT[b], s]).wait()

    def meta_hop(source, target):
        offset = tuple((q - p) % 4 for p, q in zip(OFFSETS[source], OFFSETS[target]))
        c = pltpu.make_async_remote_copy(
            src_ref=meta.at[SLOT[source], core], dst_ref=meta.at[SLOT[target], core],
            send_sem=m_send.at[SLOT[target]], recv_sem=m_recv.at[SLOT[target]],
            device_id=device(offset, core), device_id_type=MESH)
        c.start()
        pending.append(c)

    def meta_got(b):
        here = meta.at[SLOT[b], core]
        pltpu.make_async_copy(here, here, m_recv.at[SLOT[b]]).wait()

    def meta_share(b):
        here = meta.at[SLOT[b], core]
        c = pltpu.make_async_remote_copy(
            src_ref=here, dst_ref=here, send_sem=md_send.at[SLOT[b]], recv_sem=md_recv.at[SLOT[b]],
            device_id=sibling, device_id_type=MESH)
        c.start()
        pending.append(c)

    def meta_shared(b):
        here = meta.at[SLOT[b], 1 - core]
        pltpu.make_async_copy(here, here, md_recv.at[SLOT[b]]).wait()

    def share(b, s):
        c = pltpu.make_async_remote_copy(
            src_ref=place(b, s), dst_ref=place(b, s),
            send_sem=d2d_send.at[SLOT[b], s], recv_sem=d2d_recv.at[SLOT[b], s],
            device_id=sibling, device_id_type=MESH)
        c.start()
        pending.append(c)

    def shared(b):
        for s in range(CHUNKS):
            here = full.at[SLOT[b], pl.ds(pl.multiple_of((1 - core) * rows + s * step, step), step)]
            pltpu.make_async_copy(here, here, d2d_recv.at[SLOT[b], s]).wait()

    def columns(b):
        r = meta[SLOT[b], core]
        r = r[:, 0:384] + r[:, 320:704]
        t = jnp.transpose(jnp.broadcast_to(r, (128, 384)))[:rows]
        col_g[SLOT[b]] = t
        col_c[SLOT[b]] = jnp.floor(t * (1.0 / scale))

    def tiles(j, others):
        left = full[SLOT[j], pl.ds(mine, rows), :] if j in FULL else half[SLOT[j] - len(FULL)]
        cj, gj = col_c[SLOT[j]], col_g[SLOT[j]]
        best = acc_row[SLOT[j]]
        for i in others:
            sims = lax.dot_general(left, full[SLOT[i]], NT, preferred_element_type=jnp.float32)
            gi = meta[SLOT[i], 0] + meta[SLOT[i], 1]
            ci = jnp.floor(gi * (1.0 / scale))
            for n in range(0, pair_rows, 128):
                t = jnp.where(cj == ci[:, n:n + 128], sims[:, n:n + 128], -1.0)
                earlier = gi[:, n:n + 128] < gj
                best = jnp.maximum(best, jnp.where(earlier, t, -1.0))
                if j + i not in ONE_WAY:
                    u = jnp.max(jnp.where(earlier, -1.0, t).reshape(rows // 8, 8, 128), axis=0)
                    acc_col[SLOT[i], :, n:n + 128] = jnp.maximum(acc_col[SLOT[i], :, n:n + 128], u)
        acc_row[SLOT[j]] = best

    lanes = lax.broadcasted_iota(jnp.int32, (1, pair_rows), 1)
    ours = (lanes >= core * rows) & (lanes < (core + 1) * rows)

    def summary(b):
        m = jnp.full((1, pair_rows), -1.0, jnp.float32)
        if b not in "f":
            a = acc_row[SLOT[b]]
            a = jnp.concatenate([a, jnp.full((384 - rows, 128), -1.0, jnp.float32)], axis=0)
            r = jnp.max(jnp.transpose(a), axis=0, keepdims=True)[:, :rows]
            m = jnp.where(ours, jnp.concatenate([r, r], axis=1), m)
        if b in COLUMNS:
            m = jnp.maximum(m, jnp.max(acc_col[SLOT[b]], axis=0, keepdims=True))
        return m

    def give(b):
        n = RETURNED.index(b)
        back[n] = summary(b)
        for which in ((0, 1) if b in FULL else (0,)):
            target = core if which == 0 else 1 - core
            c = pltpu.make_async_remote_copy(
                src_ref=back.at[n], dst_ref=ret.at[which, n],
                send_sem=r_send.at[which, n], recv_sem=r_recv.at[which, n],
                device_id=device(minus(OFFSETS[b]), target), device_id_type=MESH)
            c.start()
            pending.append(c)

    values = x_ref[...].astype(jnp.float32)
    units = values * lax.rsqrt(jnp.sum(values * values, axis=1, keepdims=True) + epsilon)
    full[0, pl.ds(mine, rows), :] = units.astype(jnp.bfloat16)
    wide = lax.broadcasted_iota(jnp.int32, (1, 768), 1)
    meta[0, core] = jnp.where((wide >= core * rows) & (wide < (core + 1) * rows), meta_in[...], 0.0)
    pl.semaphore_wait(barrier, len(neighbours))

    for b in "fcag":
        meta_hop("o", b)
    meta_share("o")
    for s in range(CHUNKS):
        for b in "fcag":
            hop("o", b, s)
    for s in range(CHUNKS):
        share("o", s)
    acc_row[...] = jnp.full_like(acc_row, -1.0)
    acc_col[...] = jnp.full_like(acc_col, -1.0)
    columns("o")
    meta_shared("o")
    shared("o")
    for b, children in (("f", "k"), ("c", "ed"), ("a", "b"), ("g", "h")):
        meta_got(b)
        for t in children:
            meta_hop(b, t)
        meta_share(b)
        if b != "f":
            columns(b)
    tiles("o", "o")
    meta_got("e")
    meta_hop("e", "j")
    meta_got("h")
    meta_hop("h", "i")
    meta_share("e")
    meta_share("h")
    for b in "kbd":
        meta_got(b)
        meta_share(b)
    for s in range(CHUNKS):
        got("f", s)
        hop("f", "k", s)
        got("c", s)
        hop("c", "e", s)
        share("f", s)
        share("c", s)
        got("a", s)
        got("g", s)
        share("a", s)
        share("g", s)
        if s >= 3:
            for r in ((0, 1) if s == 3 else (2, 3, 4)):
                hop("a", "b", r)
                hop("g", "h", r)
                if r < 3:
                    hop("c", "d", r)
    for b in "acgf":
        meta_shared(b)
        shared(b)
    tiles("o", "acg")
    for s in range(CHUNKS):
        got("e", s)
        share("e", s)
        hop("e", "j", s)
        if s >= 3:
            hop("e", "d", s)
    tiles("a", "cgf")
    got("h", 0)
    hop("h", "i", 0)
    for s in range(CHUNKS):
        got("k", s)
        share("k", s)
    tiles("g", "cf")
    tiles("c", "f")
    for b in "ek":
        columns(b)
        meta_shared(b)
        shared(b)
    tiles("k", "acge")
    got("h", 1)
    hop("h", "i", 1)
    tiles("e", "fga")
    got("h", 2)
    hop("h", "i", 2)
    columns("d")
    meta_shared("d")
    for s in range(CHUNKS):
        got("d", s)
        share("d", s)
    shared("d")
    tiles("d", "fkgc")
    got("h", 3)
    hop("h", "i", 3)
    columns("b")
    columns("h")
    for b in "bhij":
        if b in "bh":
            meta_shared(b)
        else:
            meta_got(b)
            columns(b)
    got("h", 4)
    hop("h", "i", 4)
    for s in range(CHUNKS):
        share("h", s)
        got("b", s)
        share("b", s)
    shared("b")
    shared("h")
    tiles("b", "gkh")
    tiles("h", "aeod")
    for b in "gkd":
        give(b)
    for s in range(CHUNKS):
        got("j", s)
    tiles("j", "bcfh")
    for s in range(CHUNKS):
        got("i", s)
    tiles("i", "acde")
    for b in "bcfhjaei":
        give(b)
    total = summary("o")
    for c in pending:
        c.wait_send()
    for n, b in enumerate(RETURNED):
        for which in ((0, 1) if b in FULL else (0,)):
            here = ret.at[which, n]
            pltpu.make_async_copy(here, here, r_recv.at[which, n]).wait()
            total = jnp.maximum(total, ret[which, n])
    out_ref[...] = jnp.where(core == 0, total[:, :rows], total[:, rows:])


def shards(embeddings, cluster, order_key):
    rows, width = embeddings.shape
    both = (cluster[:, 0] * 65536 + order_key).astype(jnp.float32)
    both = jnp.concatenate([both, both, jnp.zeros((768 - 2 * rows,), jnp.float32)]).reshape(1, 768)
    nf, nh, nb, nr = len(FULL), len(HALF), len(BLOCKS), len(RETURNED)

    dma = pltpu.SemaphoreType.DMA
    best = pl.pallas_call(
        functools.partial(kernel, rows, width),
        out_shape=jax.ShapeDtypeStruct((1, rows), jnp.float32),
        in_specs=[pl.BlockSpec(memory_space=pltpu.VMEM)] * 2,
        out_specs=pl.BlockSpec(memory_space=pltpu.VMEM),
        scratch_shapes=[
            pltpu.VMEM((nf, 2 * rows, width), jnp.bfloat16),
            pltpu.VMEM((nh, rows, width), jnp.bfloat16),
            pltpu.VMEM((nb, 2, 1, 768), jnp.float32),
            pltpu.VMEM((nb, rows, 128), jnp.float32),
            pltpu.VMEM((nb, rows, 128), jnp.float32),
            pltpu.VMEM((nb, rows, 128), jnp.float32),
            pltpu.VMEM((nf, 8, 2 * rows), jnp.float32),
            pltpu.VMEM((2, nr, 1, 2 * rows), jnp.float32),
            pltpu.VMEM((nr, 1, 2 * rows), jnp.float32),
            dma((nb, CHUNKS)), dma((nb, CHUNKS)), dma((nf, CHUNKS)), dma((nf, CHUNKS)),
            dma((nb,)), dma((nb,)), dma((nf,)), dma((nf,)), dma((2, nr)), dma((2, nr)),
        ],
        compiler_params=pltpu.CompilerParams(
            collective_id=0, has_side_effects=True, vmem_limit_bytes=56 << 20),
        cost_estimate=pl.CostEstimate(
            flops=36 * 2 * rows * 2 * rows * width, bytes_accessed=rows * width * 2, transcendentals=rows),
    )(embeddings, both)
    return best.reshape(rows)


def solution(mesh):
    placed = (P(("dp", "grid"), None), P(("dp", "grid"), None), P(("dp", "grid")))
    return jax.shard_map(
        shards, mesh=mesh, in_specs=placed, out_specs=P(("dp", "grid")), check_vma=False
    )
```

```python
import functools

import jax
import jax.numpy as jnp
from jax import lax
from jax.experimental import pallas as pl
from jax.experimental.pallas import tpu as pltpu
from jax.sharding import PartitionSpec as P

MESH = pl.DeviceIdType.MESH
NT = (((1,), (1,)), ((), ()))
epsilon = 1e-06
scale = 65536.0

OFFSETS = {
    "o": (0, 0, 0), "a": (0, 0, 1), "b": (0, 0, 3), "c": (0, 1, 0),
    "d": (0, 2, 1), "e": (0, 3, 1), "f": (1, 0, 1), "g": (1, 0, 2),
    "h": (2, 0, 1), "i": (3, 1, 0), "j": (3, 1, 3), "k": (3, 2, 0),
}
FULL = "oabcefhijk"
HALF = "dg"
CHUNKS = (80, 80, 80, 80)
ONE_WAY = {"ab", "da", "db", "dh", "gk", "ha", "hb", "oo"}
ROWS_OF = "oabcdefghijk"
COLUMNS_OF = "oabcefij"
PROGRAM = (
    ">oc0", ">oa0", ">ob0", ">oc1", ">oa1", ">ob1", ">oc2", ">oa2", ">ob2", ">oc3", ">oa3", ">ob3", "=o0", "=o1",
    "=o2", "=o3", "!o", "*oo", "?c0", ">ci0", "=c0", "?a0", ">af0", ">ae0", "=a0", "?b0", "=b0", "?c1", ">ci1",
    "=c1", "?a1", ">af1", ">ae1", "=a1", "?b1", "=b1", "?i0", ">ik0", ">ij0", "=i0", "?f0", ">fg0", "=f0", "?e0",
    "=e0", "?c2", ">ci2", "=c2", "?a2", ">af2", ">ae2", "=a2", "?b2", "=b2", "?i1", ">ik1", ">ij1", "=i1", "?f1",
    ">fg1", "=f1", "?e1", "=e1", "?c3", ">ci3", "=c3", "?a3", ">af3", ">ae3", ">fh0", ">ed0", ">fh1", ">ed1", "=a3",
    "?b3", "=b3", "*co", "!c", "*bc", "?i2", ">ik2", ">ij2", "=i2", "?f2", ">fh2", ">fg2", "=f2", "?e2", ">ed2",
    "=e2", "?k0", "=k0", "?g0", "?j0", "=j0", "!b", "*aocb", "?i3", ">ik3", ">ij3", "=i3", "?f3", ">fh3", ">fg3",
    "=f3", "?e3", ">ed3", "=e3", "?k1", "=k1", "?g1", "?j1", "=j1", "!a", "*ioab", "!i", "*fobai", "?h0", "=h0",
    "?d0", "?k2", "=k2", "?g2", "?j2", "=j2", "!f", "*ecibf", "<c", "?h1", "=h1", "?d1", "?k3", "=k3", "?g3", "?j3",
    "=j3", "*kobf", "!e", "*jaef", "<f", "?h2", "=h2", "?d2", "!j", "!k", "*gbejk", "<g", "<k", "?h3", "=h3", "?d3",
    "*hoabei", "<e", "<i", "!h", "*dabhj", "<a", "<b", "<d", "<h", "<j",
)
BLOCKS = FULL + HALF
SLOT = {b: n for n, b in enumerate(BLOCKS)}


def kernel(rows, width, x_ref, cluster_ref, key_ref, out_ref, full, half, meta, col_c, col_g, acc_row, acc_col, ret, back,
           send, recv, d2d_send, d2d_recv, m_send, m_recv, md_send, md_recv, r_send, r_recv):
    x, grid = lax.axis_index("dp"), lax.axis_index("grid")
    y, z, core = grid // 8, (grid // 2) % 4, grid % 2
    pair_rows = 2 * rows
    starts = [sum(CHUNKS[:n]) for n in range(len(CHUNKS))]
    mine = pl.multiple_of(core * rows, 16)

    def device(offset, which):
        dx, dy, dz = offset
        return ((x + dx) % 4, ((y + dy) % 4) * 8 + ((z + dz) % 4) * 2 + which)

    sibling = device((0, 0, 0), 1 - core)
    barrier = pltpu.get_barrier_semaphore()
    partners = {((0, 0, 0), 1)}
    for b in BLOCKS[1:]:
        for offset in (OFFSETS[b], tuple(-v % 4 for v in OFFSETS[b])):
            partners.add((offset, 0))
            if b in FULL:
                partners.add((offset, 1))
    partners = [device(offset, 1 - core if other else core) for offset, other in sorted(partners)]
    for n in partners:
        pl.semaphore_signal(barrier, inc=1, device_id=n, device_id_type=MESH)

    pending = []

    def copy(src, dst, send_sem, recv_sem, to):
        c = pltpu.make_async_remote_copy(
            src_ref=src, dst_ref=dst, send_sem=send_sem, recv_sem=recv_sem, device_id=to, device_id_type=MESH)
        c.start()
        pending.append(c)

    def arrived(here, sem):
        pltpu.make_async_copy(here, here, sem).wait()

    def place(b, s, which):
        if b in FULL:
            return full.at[SLOT[b], pl.ds(pl.multiple_of(which * rows + starts[s], 16), CHUNKS[s])]
        return half.at[SLOT[b] - len(FULL), pl.ds(starts[s], CHUNKS[s])]

    def hop(source, target, s):
        offset = tuple((q - p) % 4 for p, q in zip(OFFSETS[source], OFFSETS[target]))
        a, b, to = SLOT[source], SLOT[target], device(offset, core)
        if s == 0:
            copy(meta.at[a, core], meta.at[b, core], m_send.at[b], m_recv.at[b], to)
        copy(place(source, s, core), place(target, s, core), send.at[b, s], recv.at[b, s], to)

    def got(b, s):
        n = SLOT[b]
        if s == 0:
            arrived(meta.at[n, core], m_recv.at[n])
        arrived(place(b, s, core), recv.at[n, s])

    def share(b, s):
        n = SLOT[b]
        if s == 0:
            copy(meta.at[n, core], meta.at[n, core], md_send.at[n], md_recv.at[n], sibling)
        copy(place(b, s, core), place(b, s, core), d2d_send.at[n, s], d2d_recv.at[n, s], sibling)

    def shared(b):
        n = SLOT[b]
        arrived(meta.at[n, 1 - core], md_recv.at[n])
        for s in range(len(CHUNKS)):
            arrived(place(b, s, 1 - core), d2d_recv.at[n, s])

    def columns(b):
        r = meta[SLOT[b], core]
        r = r[:, 0:384] + r[:, 320:704]
        t = jnp.transpose(jnp.broadcast_to(r, (128, 384)))[:rows]
        col_g[SLOT[b]] = t
        col_c[SLOT[b]] = jnp.floor(t * (1.0 / scale))

    def tiles(j, others):
        left = full[SLOT[j], pl.ds(mine, rows), :] if j in FULL else half[SLOT[j] - len(FULL)]
        cj, gj = col_c[SLOT[j]], col_g[SLOT[j]]
        best = acc_row[SLOT[j]]
        for i in others:
            sims = lax.dot_general(left, full[SLOT[i]], NT, preferred_element_type=jnp.float32)
            gi = meta[SLOT[i], 0] + meta[SLOT[i], 1]
            ci = jnp.floor(gi * (1.0 / scale))
            for n in range(0, pair_rows, 128):
                t = jnp.where(cj == ci[:, n:n + 128], sims[:, n:n + 128], -1.0)
                earlier = gi[:, n:n + 128] < gj
                best = jnp.maximum(best, jnp.where(earlier, t, -1.0))
                if j + i not in ONE_WAY:
                    u = jnp.max(jnp.where(earlier, -1.0, t).reshape(rows // 8, 8, 128), axis=0)
                    acc_col[SLOT[i], :, n:n + 128] = jnp.maximum(acc_col[SLOT[i], :, n:n + 128], u)
        acc_row[SLOT[j]] = best

    lanes = lax.broadcasted_iota(jnp.int32, (1, pair_rows), 1)
    ours = (lanes >= core * rows) & (lanes < (core + 1) * rows)

    def summary(b):
        m = jnp.full((1, pair_rows), -1.0, jnp.float32)
        if b in ROWS_OF:
            a = jnp.concatenate([acc_row[SLOT[b]], jnp.full((384 - rows, 128), -1.0, jnp.float32)], axis=0)
            r = jnp.max(jnp.transpose(a), axis=0, keepdims=True)[:, :rows]
            m = jnp.where(ours, jnp.concatenate([r, r], axis=1), m)
        if b in COLUMNS_OF:
            m = jnp.maximum(m, jnp.max(acc_col[SLOT[b]], axis=0, keepdims=True))
        return m

    def owners(b):
        return (1,) if b == "o" else (0, 1) if b in COLUMNS_OF else (0,)

    def give(b):
        n = SLOT[b]
        back[n] = summary(b)
        home = tuple(-v for v in OFFSETS[b])
        for which in owners(b):
            copy(back.at[n], ret.at[which, n], r_send.at[which, n], r_recv.at[which, n],
                 device(home, 1 - core if which else core))

    values = x_ref[...].astype(jnp.float32)
    units = values * lax.rsqrt(jnp.sum(values * values, axis=1, keepdims=True) + epsilon)
    full[0, pl.ds(mine, rows), :] = units.astype(jnp.bfloat16)
    wide = lax.broadcasted_iota(jnp.int32, (1, 768), 1)
    own = (cluster_ref[...] * 65536 + key_ref[...].reshape(1, rows)).astype(jnp.float32)
    own = jnp.concatenate([own, own, jnp.zeros((1, 768 - 2 * rows), jnp.float32)], axis=1)
    meta[0, core] = jnp.where((wide >= core * rows) & (wide < (core + 1) * rows), own, 0.0)
    pl.semaphore_wait(barrier, len(partners))

    known = set()
    for token in PROGRAM:
        what, b = token[0], token[1]
        if what == ">":
            hop(b, token[2], int(token[3]))
        elif what == "?":
            got(b, int(token[2]))
        elif what == "=":
            share(b, int(token[2]))
        elif what == "!":
            if b == "o":
                acc_row[...] = jnp.full_like(acc_row, -1.0)
                acc_col[...] = jnp.full_like(acc_col, -1.0)
            shared(b)
        elif what == "*":
            if b not in known:
                columns(b)
                known.add(b)
            tiles(b, token[2:])
        else:
            give(b)
    if "o" in COLUMNS_OF:
        give("o")
    total = back[0]
    for c in pending:
        c.wait_send()
    for b in BLOCKS:
        for which in owners(b):
            arrived(ret.at[which, SLOT[b]], r_recv.at[which, SLOT[b]])
            total = jnp.maximum(total, ret[which, SLOT[b]])
    out_ref[...] = jnp.where(core == 0, total[:, :rows], total[:, rows:]).reshape(rows)


def shards(embeddings, cluster, order_key):
    rows, width = embeddings.shape
    nf, nh, nb, nc = len(FULL), len(HALF), len(BLOCKS), len(CHUNKS)
    dma = pltpu.SemaphoreType.DMA
    return pl.pallas_call(
        functools.partial(kernel, rows, width),
        out_shape=jax.ShapeDtypeStruct((rows,), jnp.float32),
        in_specs=[pl.BlockSpec(memory_space=pltpu.VMEM)] * 3,
        out_specs=pl.BlockSpec(memory_space=pltpu.VMEM),
        scratch_shapes=[
            pltpu.VMEM((nf, 2 * rows, width), jnp.bfloat16),
            pltpu.VMEM((nh, rows, width), jnp.bfloat16),
            pltpu.VMEM((nb, 2, 1, 768), jnp.float32),
            pltpu.VMEM((nb, rows, 128), jnp.float32),
            pltpu.VMEM((nb, rows, 128), jnp.float32),
            pltpu.VMEM((nb, rows, 128), jnp.float32),
            pltpu.VMEM((nf, 8, 2 * rows), jnp.float32),
            pltpu.VMEM((2, nb, 1, 2 * rows), jnp.float32),
            pltpu.VMEM((nb, 1, 2 * rows), jnp.float32),
            dma((nb, nc)), dma((nb, nc)), dma((nf, nc)), dma((nf, nc)),
            dma((nb,)), dma((nb,)), dma((nf,)), dma((nf,)), dma((2, nb)), dma((2, nb)),
        ],
        compiler_params=pltpu.CompilerParams(
            collective_id=0, has_side_effects=True, vmem_limit_bytes=56 << 20),
        cost_estimate=pl.CostEstimate(
            flops=36 * 2 * rows * 2 * rows * width, bytes_accessed=rows * width * 2, transcendentals=rows),
    )(embeddings, cluster.reshape(1, rows), order_key)


def solution(mesh):
    placed = (P(("dp", "grid"), None), P(("dp", "grid"), None), P(("dp", "grid")))
    return jax.shard_map(
        shards, mesh=mesh, in_specs=placed, out_specs=P(("dp", "grid")), check_vma=False
    )
```

```python
import functools

import jax
import jax.numpy as jnp
from jax import lax
from jax.experimental import pallas as pl
from jax.experimental.pallas import tpu as pltpu
from jax.sharding import PartitionSpec as P

MESH = pl.DeviceIdType.MESH
NT = (((1,), (1,)), ((), ()))
epsilon = 1e-06
scale = 65536.0

OFFSETS = {
    "o": (0, 0, 0), "a": (0, 0, 1), "b": (0, 0, 3), "c": (0, 1, 0),
    "d": (0, 2, 1), "e": (0, 3, 1), "f": (1, 0, 1), "g": (1, 0, 2),
    "h": (2, 0, 1), "i": (3, 1, 0), "j": (3, 1, 3), "k": (3, 2, 0),
}
FULL = "oabcefhijk"
HALF = "dg"
CHUNKS = (80, 80, 80, 80)
ONE_WAY = {"ab", "da", "db", "dh", "gk", "ha", "hb", "oo"}
ROWS_OF = "oabcdefghijk"
COLUMNS_OF = "oabcefij"
PROGRAM = (
    ">oc0", ">oa0", ">ob0", ">oc1", ">oa1", ">ob1", ">oc2", ">oa2", ">ob2", ">oc3", ">oa3", ">ob3", "=o0", "=o1",
    "=o2", "=o3", "!o", "*oo", "?c0", ">ci0", "=c0", "?a0", ">af0", ">ae0", "=a0", "?b0", "=b0", "?c1", ">ci1",
    "=c1", "?a1", ">af1", ">ae1", "=a1", "?b1", "=b1", "?i0", ">ik0", ">ij0", "=i0", "?f0", ">fg0", "=f0", "?e0",
    "=e0", "?c2", ">ci2", "=c2", "?a2", ">af2", ">ae2", "=a2", "?b2", "=b2", "?i1", ">ik1", ">ij1", "=i1", "?f1",
    ">fg1", "=f1", "?e1", "=e1", "?c3", ">ci3", "=c3", "?a3", ">af3", ">ae3", ">fh0", ">ed0", ">fh1", ">ed1", "=a3",
    "?b3", "=b3", "*co", "!c", "*bc", "?i2", ">ik2", ">ij2", "=i2", "?f2", ">fh2", ">fg2", "=f2", "?e2", ">ed2",
    "=e2", "?k0", "=k0", "?g0", "?j0", "=j0", "!b", "*aocb", "?i3", ">ik3", ">ij3", "=i3", "?f3", ">fh3", ">fg3",
    "=f3", "?e3", ">ed3", "=e3", "?k1", "=k1", "?g1", "?j1", "=j1", "!a", "*ioab", "!i", "*fobai", "?h0", "=h0",
    "?d0", "?k2", "=k2", "?g2", "?j2", "=j2", "!f", "*ecibf", "<c", "?h1", "=h1", "?d1", "?k3", "=k3", "?g3", "?j3",
    "=j3", "*kobf", "!e", "*jaef", "<f", "?h2", "=h2", "?d2", "!j", "!k", "*gbejk", "<g", "<k", "?h3", "=h3", "?d3",
    "*hoabei", "<e", "<i", "!h", "*dabhj", "<a", "<b", "<d", "<h", "<j",
)
BLOCKS = FULL + HALF
SLOT = {b: n for n, b in enumerate(BLOCKS)}


def kernel(rows, width, x_hbm, cluster_ref, key_ref, out_ref, x_ref, x_sem, full, half, meta, col_c, col_g, acc_row, acc_col, ret, back,
           send, recv, d2d_send, d2d_recv, m_send, m_recv, md_send, md_recv, r_send, r_recv):
    x, grid = lax.axis_index("dp"), lax.axis_index("grid")
    y, z, core = grid // 8, (grid // 2) % 4, grid % 2
    pair_rows = 2 * rows
    starts = [sum(CHUNKS[:n]) for n in range(len(CHUNKS))]
    mine = pl.multiple_of(core * rows, 16)

    def device(offset, which):
        dx, dy, dz = offset
        return ((x + dx) % 4, ((y + dy) % 4) * 8 + ((z + dz) % 4) * 2 + which)

    sibling = device((0, 0, 0), 1 - core)
    load = pltpu.make_async_copy(x_hbm, x_ref, x_sem)
    load.start()
    barrier = pltpu.get_barrier_semaphore()
    partners = {((0, 0, 0), 1)}
    for b in BLOCKS[1:]:
        for offset in (OFFSETS[b], tuple(-v % 4 for v in OFFSETS[b])):
            partners.add((offset, 0))
            if b in FULL:
                partners.add((offset, 1))
    partners = [device(offset, 1 - core if other else core) for offset, other in sorted(partners)]
    for n in partners:
        pl.semaphore_signal(barrier, inc=1, device_id=n, device_id_type=MESH)

    pending = []

    def copy(src, dst, send_sem, recv_sem, to):
        c = pltpu.make_async_remote_copy(
            src_ref=src, dst_ref=dst, send_sem=send_sem, recv_sem=recv_sem, device_id=to, device_id_type=MESH)
        c.start()
        pending.append(c)

    def arrived(here, sem):
        pltpu.make_async_copy(here, here, sem).wait()

    def place(b, s, which):
        if b in FULL:
            return full.at[SLOT[b], pl.ds(pl.multiple_of(which * rows + starts[s], 16), CHUNKS[s])]
        return half.at[SLOT[b] - len(FULL), pl.ds(starts[s], CHUNKS[s])]

    def hop(source, target, s):
        offset = tuple((q - p) % 4 for p, q in zip(OFFSETS[source], OFFSETS[target]))
        a, b, to = SLOT[source], SLOT[target], device(offset, core)
        if s == 0:
            copy(meta.at[a, core], meta.at[b, core], m_send.at[b], m_recv.at[b], to)
        copy(place(source, s, core), place(target, s, core), send.at[b, s], recv.at[b, s], to)

    def got(b, s):
        n = SLOT[b]
        if s == 0:
            arrived(meta.at[n, core], m_recv.at[n])
        arrived(place(b, s, core), recv.at[n, s])

    def share(b, s):
        n = SLOT[b]
        if s == 0:
            copy(meta.at[n, core], meta.at[n, core], md_send.at[n], md_recv.at[n], sibling)
        copy(place(b, s, core), place(b, s, core), d2d_send.at[n, s], d2d_recv.at[n, s], sibling)

    def shared(b):
        n = SLOT[b]
        arrived(meta.at[n, 1 - core], md_recv.at[n])
        for s in range(len(CHUNKS)):
            arrived(place(b, s, 1 - core), d2d_recv.at[n, s])

    def columns(b):
        r = meta[SLOT[b], core]
        r = r[:, 0:384] + r[:, 320:704]
        t = jnp.transpose(jnp.broadcast_to(r, (128, 384)))[:rows]
        col_g[SLOT[b]] = t
        col_c[SLOT[b]] = jnp.floor(t * (1.0 / scale))

    def tiles(j, others):
        left = full[SLOT[j], pl.ds(mine, rows), :] if j in FULL else half[SLOT[j] - len(FULL)]
        cj, gj = col_c[SLOT[j]], col_g[SLOT[j]]
        best = acc_row[SLOT[j]]
        keys = {i: meta[SLOT[i], 0] + meta[SLOT[i], 1] for i in others}
        groups = {i: jnp.floor(keys[i] * (1.0 / scale)) for i in others}
        units = [(i, n) for i in others for n in range(0, pair_rows, 128)]
        for first in range(0, len(units), 2):
            some = units[first:first + 2]
            right = [full[SLOT[i], n:n + 128, :] for i, n in some]
            right = right[0] if len(some) == 1 else jnp.concatenate(right, axis=0)
            sims = lax.dot_general(left, right, NT, preferred_element_type=jnp.float32)
            for at, (i, n) in enumerate(some):
                t = jnp.where(cj == groups[i][:, n:n + 128], sims[:, at * 128:at * 128 + 128], -1.0)
                earlier = keys[i][:, n:n + 128] < gj
                best = jnp.maximum(best, jnp.where(earlier, t, -1.0))
                if j + i not in ONE_WAY:
                    u = jnp.max(jnp.where(earlier, -1.0, t).reshape(rows // 8, 8, 128), axis=0)
                    acc_col[SLOT[i], :, n:n + 128] = jnp.maximum(acc_col[SLOT[i], :, n:n + 128], u)
        acc_row[SLOT[j]] = best

    lanes = lax.broadcasted_iota(jnp.int32, (1, pair_rows), 1)
    ours = (lanes >= core * rows) & (lanes < (core + 1) * rows)

    def summary(b):
        m = jnp.full((1, pair_rows), -1.0, jnp.float32)
        if b in ROWS_OF:
            a = jnp.concatenate([acc_row[SLOT[b]], jnp.full((384 - rows, 128), -1.0, jnp.float32)], axis=0)
            r = jnp.max(jnp.transpose(a), axis=0, keepdims=True)[:, :rows]
            m = jnp.where(ours, jnp.concatenate([r, r], axis=1), m)
        if b in COLUMNS_OF:
            m = jnp.maximum(m, jnp.max(acc_col[SLOT[b]], axis=0, keepdims=True))
        return m

    def owners(b):
        return (1,) if b == "o" else (0, 1) if b in COLUMNS_OF else (0,)

    def give(b):
        n = SLOT[b]
        back[n] = summary(b)
        home = tuple(-v for v in OFFSETS[b])
        for which in owners(b):
            copy(back.at[n], ret.at[which, n], r_send.at[which, n], r_recv.at[which, n],
                 device(home, 1 - core if which else core))

    load.wait()
    values = x_ref[...].astype(jnp.float32)
    units = values * lax.rsqrt(jnp.sum(values * values, axis=1, keepdims=True) + epsilon)
    full[0, pl.ds(mine, rows), :] = units.astype(jnp.bfloat16)
    wide = lax.broadcasted_iota(jnp.int32, (1, 768), 1)
    own = (cluster_ref[...] * 65536 + key_ref[...].reshape(1, rows)).astype(jnp.float32)
    own = jnp.concatenate([own, own, jnp.zeros((1, 768 - 2 * rows), jnp.float32)], axis=1)
    meta[0, core] = jnp.where((wide >= core * rows) & (wide < (core + 1) * rows), own, 0.0)
    pl.semaphore_wait(barrier, len(partners))

    known = set()
    for token in PROGRAM:
        what, b = token[0], token[1]
        if what == ">":
            hop(b, token[2], int(token[3]))
        elif what == "?":
            got(b, int(token[2]))
        elif what == "=":
            share(b, int(token[2]))
        elif what == "!":
            if b == "o":
                acc_row[...] = jnp.full_like(acc_row, -1.0)
                acc_col[...] = jnp.full_like(acc_col, -1.0)
            shared(b)
        elif what == "*":
            if b not in known:
                columns(b)
                known.add(b)
            tiles(b, token[2:])
        else:
            give(b)
    if "o" in COLUMNS_OF:
        give("o")
    total = back[0]
    for c in pending:
        c.wait_send()
    for b in BLOCKS:
        for which in owners(b):
            arrived(ret.at[which, SLOT[b]], r_recv.at[which, SLOT[b]])
            total = jnp.maximum(total, ret[which, SLOT[b]])
    out_ref[...] = jnp.where(core == 0, total[:, :rows], total[:, rows:]).reshape(rows)


def shards(embeddings, cluster, order_key):
    rows, width = embeddings.shape
    nf, nh, nb, nc = len(FULL), len(HALF), len(BLOCKS), len(CHUNKS)
    dma = pltpu.SemaphoreType.DMA
    return pl.pallas_call(
        functools.partial(kernel, rows, width),
        out_shape=jax.ShapeDtypeStruct((rows,), jnp.float32),
        in_specs=[pl.BlockSpec(memory_space=pl.ANY)] + [pl.BlockSpec(memory_space=pltpu.VMEM)] * 2,
        out_specs=pl.BlockSpec(memory_space=pltpu.VMEM),
        scratch_shapes=[
            pltpu.VMEM((rows, width), jnp.bfloat16),
            pltpu.SemaphoreType.DMA,
            pltpu.VMEM((nf, 2 * rows, width), jnp.bfloat16),
            pltpu.VMEM((nh, rows, width), jnp.bfloat16),
            pltpu.VMEM((nb, 2, 1, 768), jnp.float32),
            pltpu.VMEM((nb, rows, 128), jnp.float32),
            pltpu.VMEM((nb, rows, 128), jnp.float32),
            pltpu.VMEM((nb, rows, 128), jnp.float32),
            pltpu.VMEM((nf, 8, 2 * rows), jnp.float32),
            pltpu.VMEM((2, nb, 1, 2 * rows), jnp.float32),
            pltpu.VMEM((nb, 1, 2 * rows), jnp.float32),
            dma((nb, nc)), dma((nb, nc)), dma((nf, nc)), dma((nf, nc)),
            dma((nb,)), dma((nb,)), dma((nf,)), dma((nf,)), dma((2, nb)), dma((2, nb)),
        ],
        compiler_params=pltpu.CompilerParams(
            collective_id=0, has_side_effects=True, vmem_limit_bytes=56 << 20),
        cost_estimate=pl.CostEstimate(
            flops=36 * 2 * rows * 2 * rows * width, bytes_accessed=rows * width * 2, transcendentals=rows),
    )(embeddings, cluster.reshape(1, rows), order_key)


def solution(mesh):
    placed = (P(("dp", "grid"), None), P(("dp", "grid"), None), P(("dp", "grid")))
    return jax.shard_map(
        shards, mesh=mesh, in_specs=placed, out_specs=P(("dp", "grid")), check_vma=False
    )
```

```python
import functools

import jax
import jax.numpy as jnp
from jax import lax
from jax.experimental import pallas as pl
from jax.experimental.pallas import tpu as pltpu
from jax.sharding import PartitionSpec as P

MESH = pl.DeviceIdType.MESH
NT = (((1,), (1,)), ((), ()))
epsilon = 1e-06
scale = 65536.0

OFFSETS = {
    "o": (0, 0, 0), "a": (0, 0, 1), "b": (0, 0, 3), "c": (0, 1, 0),
    "d": (0, 2, 1), "e": (0, 3, 1), "f": (1, 0, 1), "g": (1, 0, 2),
    "h": (2, 0, 1), "i": (3, 1, 0), "j": (3, 1, 3), "k": (3, 2, 0),
}
FULL = "oabcefhijk"
HALF = "dg"
CHUNKS = (80, 80, 80, 80)
ONE_WAY = {"ab", "da", "db", "dh", "gk", "ha", "hb", "oo"}
ROWS_OF = "oabcdefghijk"
COLUMNS_OF = "oabcefij"
PROGRAM = (
    ">oc0", ">oa0", ">ob0", ">oc1", ">oa1", ">ob1", ">oc2", ">oa2", ">ob2", ">oc3", ">oa3", ">ob3", "=o0", "=o1",
    "=o2", "=o3", "!o", "*oo", "?c0", ">ci0", "=c0", "?a0", ">af0", ">ae0", "=a0", "?b0", "=b0", "?c1", ">ci1",
    "=c1", "?a1", ">af1", ">ae1", "=a1", "?b1", "=b1", "?i0", ">ik0", ">ij0", "=i0", "?f0", ">fg0", "=f0", "?e0",
    "=e0", "?c2", ">ci2", "=c2", "?a2", ">af2", ">ae2", "=a2", "?b2", "=b2", "?i1", ">ik1", ">ij1", "=i1", "?f1",
    ">fg1", "=f1", "?e1", "=e1", "?c3", ">ci3", "=c3", "?a3", ">af3", ">ae3", ">fh0", ">ed0", ">fh1", ">ed1", "=a3",
    "?b3", "=b3", "*co", "!c", "*bc", "?i2", ">ik2", ">ij2", "=i2", "?f2", ">fh2", ">fg2", "=f2", "?e2", ">ed2",
    "=e2", "?k0", "=k0", "?g0", "?j0", "=j0", "!b", "*aocb", "?i3", ">ik3", ">ij3", "=i3", "?f3", ">fh3", ">fg3",
    "=f3", "?e3", ">ed3", "=e3", "?k1", "=k1", "?g1", "?j1", "=j1", "!a", "*ioab", "!i", "*fobai", "?h0", "=h0",
    "?d0", "?k2", "=k2", "?g2", "?j2", "=j2", "!f", "*ecibf", "<c", "?h1", "=h1", "?d1", "?k3", "=k3", "?g3", "?j3",
    "=j3", "*kobf", "!e", "*jaef", "<f", "?h2", "=h2", "?d2", "!j", "!k", "*gbejk", "<g", "<k", "?h3", "=h3", "?d3",
    "*hoabei", "<e", "<i", "!h", "*dabhj", "<a", "<b", "<d", "<h", "<j",
)
BLOCKS = FULL + HALF
SLOT = {b: n for n, b in enumerate(BLOCKS)}
CROSSED = sorted(ONE_WAY - {"oo"})
COLUMNS = COLUMNS_OF + "".join(sorted({i for _, i in CROSSED} - set(COLUMNS_OF)))


def between(source, target):
    return tuple((q - p) % 4 for p, q in zip(OFFSETS[source], OFFSETS[target]))


def kernel(rows, width, x_hbm, cluster_ref, key_ref, out_ref, x_ref, x_sem, full, half, meta, col_c, col_g, acc_row, acc_col, acc_cross, ret, back,
           send, recv, d2d_send, d2d_recv, m_send, m_recv, md_send, md_recv, r_send, r_recv):
    x, grid = lax.axis_index("dp"), lax.axis_index("grid")
    y, z, core = grid // 8, (grid // 2) % 4, grid % 2
    pair_rows = 2 * rows
    starts = [sum(CHUNKS[:n]) for n in range(len(CHUNKS))]
    mine = pl.multiple_of(core * rows, 16)

    def device(offset, which):
        dx, dy, dz = offset
        return ((x + dx) % 4, ((y + dy) % 4) * 8 + ((z + dz) % 4) * 2 + which)

    sibling = device((0, 0, 0), 1 - core)
    load = pltpu.make_async_copy(x_hbm, x_ref, x_sem)
    load.start()
    barrier = pltpu.get_barrier_semaphore()
    partners = {((0, 0, 0), 1)}
    for token in PROGRAM:
        if token[0] == ">":
            offset = between(token[1], token[2])
            partners |= {(offset, 0), (tuple(-v % 4 for v in offset), 0)}
    for b in BLOCKS[1:]:
        for offset in (OFFSETS[b], tuple(-v % 4 for v in OFFSETS[b])):
            partners.add((offset, 0))
            if b in COLUMNS:
                partners.add((offset, 1))
    partners = [device(offset, 1 - core if other else core) for offset, other in sorted(partners)]
    for n in partners:
        pl.semaphore_signal(barrier, inc=1, device_id=n, device_id_type=MESH)

    pending = []

    def copy(src, dst, send_sem, recv_sem, to):
        c = pltpu.make_async_remote_copy(
            src_ref=src, dst_ref=dst, send_sem=send_sem, recv_sem=recv_sem, device_id=to, device_id_type=MESH)
        c.start()
        pending.append(c)

    def arrived(here, sem):
        pltpu.make_async_copy(here, here, sem).wait()

    def place(b, s, which):
        if b in FULL:
            return full.at[SLOT[b], pl.ds(pl.multiple_of(which * rows + starts[s], 16), CHUNKS[s])]
        return half.at[SLOT[b] - len(FULL), pl.ds(starts[s], CHUNKS[s])]

    def hop(source, target, s):
        a, b, to = SLOT[source], SLOT[target], device(between(source, target), core)
        if s == 0:
            copy(meta.at[a, core], meta.at[b, core], m_send.at[b], m_recv.at[b], to)
        copy(place(source, s, core), place(target, s, core), send.at[b, s], recv.at[b, s], to)

    def got(b, s):
        n = SLOT[b]
        if s == 0:
            arrived(meta.at[n, core], m_recv.at[n])
        arrived(place(b, s, core), recv.at[n, s])

    def share(b, s):
        n = SLOT[b]
        if s == 0:
            copy(meta.at[n, core], meta.at[n, core], md_send.at[n], md_recv.at[n], sibling)
        copy(place(b, s, core), place(b, s, core), d2d_send.at[n, s], d2d_recv.at[n, s], sibling)

    def shared(b):
        n = SLOT[b]
        arrived(meta.at[n, 1 - core], md_recv.at[n])
        for s in range(len(CHUNKS)):
            arrived(place(b, s, 1 - core), d2d_recv.at[n, s])

    def columns(b):
        r = meta[SLOT[b], core]
        r = r[:, 0:384] + r[:, 320:704]
        t = jnp.transpose(jnp.broadcast_to(r, (128, 384)))[:rows]
        col_g[SLOT[b]] = t
        col_c[SLOT[b]] = jnp.floor(t * (1.0 / scale))

    low = lax.broadcasted_iota(jnp.int32, (1, 384), 1) < rows

    def turn(j, i):
        d = between(j, i)
        return (x if d[0] == 2 else y if d[1] == 2 else z) // 2

    def tiles(j, others):
        left = full[SLOT[j], pl.ds(mine, rows), :] if j in FULL else half[SLOT[j] - len(FULL)]
        cj, gj = col_c[SLOT[j]], col_g[SLOT[j]]
        best = acc_row[SLOT[j]]
        keys = {i: meta[SLOT[i], 0] + meta[SLOT[i], 1] for i in others}
        groups = {i: jnp.floor(keys[i] * (1.0 / scale)) for i in others}
        cross = {i: j + i in ONE_WAY and i != j for i in others}
        side = {i: lax.rem(core + turn(j, i), 2) for i in others if cross[i]}
        for i in side:
            r = meta[SLOT[i], side[i]]
            keys[i] = jnp.where(low, r[:, 0:384] + r[:, 320:704], -scale)
            groups[i] = jnp.floor(keys[i] * (1.0 / scale))
        units = [(i, n) for i in others for n in ((0, 128, rows - 128) if cross[i] else range(0, pair_rows, 128))]
        for first in range(0, len(units), 2):
            some = units[first:first + 2]
            right = [
                full[SLOT[i], pl.ds(pl.multiple_of(side[i] * rows + n, 16), 128), :] if cross[i]
                else full[SLOT[i], n:n + 128, :] for i, n in some]
            right = right[0] if len(some) == 1 else jnp.concatenate(right, axis=0)
            sims = lax.dot_general(left, right, NT, preferred_element_type=jnp.float32)
            for at, (i, n) in enumerate(some):
                t = jnp.where(cj == groups[i][:, n:n + 128], sims[:, at * 128:at * 128 + 128], -1.0)
                earlier = keys[i][:, n:n + 128] < gj
                best = jnp.maximum(best, jnp.where(earlier, t, -1.0))
                if i != j:
                    u = jnp.max(jnp.where(earlier, -1.0, t).reshape(rows // 8, 8, 128), axis=0)
                    if cross[i]:
                        at_ = {0: 0, 128: 128, rows - 128: 256}[n]
                        acc_cross[CROSSED.index(j + i), :, at_:at_ + 128] = u
                    else:
                        acc_col[SLOT[i], :, n:n + 128] = jnp.maximum(acc_col[SLOT[i], :, n:n + 128], u)
        acc_row[SLOT[j]] = best

    lanes = lax.broadcasted_iota(jnp.int32, (1, pair_rows), 1)
    ours = (lanes >= core * rows) & (lanes < (core + 1) * rows)

    def summary(b):
        m = jnp.full((1, pair_rows), -1.0, jnp.float32)
        if b in ROWS_OF:
            a = jnp.concatenate([acc_row[SLOT[b]], jnp.full((384 - rows, 128), -1.0, jnp.float32)], axis=0)
            r = jnp.max(jnp.transpose(a), axis=0, keepdims=True)[:, :rows]
            m = jnp.where(ours, jnp.concatenate([r, r], axis=1), m)
        if b in COLUMNS_OF:
            m = jnp.maximum(m, jnp.max(acc_col[SLOT[b]], axis=0, keepdims=True))
        for n, (j, i) in enumerate(CROSSED):
            if i == b:
                r = jnp.max(acc_cross[n], axis=0, keepdims=True)
                r = jnp.concatenate([
                    r[:, :rows - 128], jnp.maximum(r[:, rows - 128:256], r[:, 256:512 - (rows - 128)]),
                    r[:, 256 + 256 - (rows - 128):384]], axis=1)
                side = lax.rem(core + turn(j, i), 2)
                there = (lanes >= side * rows) & (lanes < (side + 1) * rows)
                m = jnp.where(there, jnp.maximum(m, jnp.concatenate([r, r], axis=1)), m)
        return m

    def owners(b):
        return (1,) if b == "o" else (0, 1) if b in COLUMNS else (0,)

    def give(b):
        n = SLOT[b]
        back[n] = summary(b)
        home = tuple(-v for v in OFFSETS[b])
        for which in owners(b):
            copy(back.at[n], ret.at[which, n], r_send.at[which, n], r_recv.at[which, n],
                 device(home, 1 - core if which else core))

    load.wait()
    values = x_ref[...].astype(jnp.float32)
    units = values * lax.rsqrt(jnp.sum(values * values, axis=1, keepdims=True) + epsilon)
    full[0, pl.ds(mine, rows), :] = units.astype(jnp.bfloat16)
    wide = lax.broadcasted_iota(jnp.int32, (1, 768), 1)
    own = (cluster_ref[...] * 65536 + key_ref[...].reshape(1, rows)).astype(jnp.float32)
    own = jnp.concatenate([own, own, jnp.zeros((1, 768 - 2 * rows), jnp.float32)], axis=1)
    meta[0, core] = jnp.where((wide >= core * rows) & (wide < (core + 1) * rows), own, 0.0)
    pl.semaphore_wait(barrier, len(partners))

    known = set()
    for token in PROGRAM:
        what, b = token[0], token[1]
        if what == ">":
            hop(b, token[2], int(token[3]))
        elif what == "?":
            got(b, int(token[2]))
        elif what == "=":
            share(b, int(token[2]))
        elif what == "!":
            if b == "o":
                acc_row[...] = jnp.full_like(acc_row, -1.0)
                acc_col[...] = jnp.full_like(acc_col, -1.0)
            shared(b)
        elif what == "*":
            if b not in known:
                columns(b)
                known.add(b)
            tiles(b, token[2:])
        else:
            give(b)
    if "o" in COLUMNS:
        give("o")
    total = back[0]
    for c in pending:
        c.wait_send()
    for b in BLOCKS:
        for which in owners(b):
            arrived(ret.at[which, SLOT[b]], r_recv.at[which, SLOT[b]])
            total = jnp.maximum(total, ret[which, SLOT[b]])
    out_ref[...] = jnp.where(core == 0, total[:, :rows], total[:, rows:]).reshape(rows)


def shards(embeddings, cluster, order_key):
    rows, width = embeddings.shape
    nf, nh, nb, nc = len(FULL), len(HALF), len(BLOCKS), len(CHUNKS)
    dma = pltpu.SemaphoreType.DMA
    return pl.pallas_call(
        functools.partial(kernel, rows, width),
        out_shape=jax.ShapeDtypeStruct((rows,), jnp.float32),
        in_specs=[pl.BlockSpec(memory_space=pl.ANY)] + [pl.BlockSpec(memory_space=pltpu.VMEM)] * 2,
        out_specs=pl.BlockSpec(memory_space=pltpu.VMEM),
        scratch_shapes=[
            pltpu.VMEM((rows, width), jnp.bfloat16),
            pltpu.SemaphoreType.DMA,
            pltpu.VMEM((nf, 2 * rows, width), jnp.bfloat16),
            pltpu.VMEM((nh, rows, width), jnp.bfloat16),
            pltpu.VMEM((nb, 2, 1, 768), jnp.float32),
            pltpu.VMEM((nb, rows, 128), jnp.float32),
            pltpu.VMEM((nb, rows, 128), jnp.float32),
            pltpu.VMEM((nb, rows, 128), jnp.float32),
            pltpu.VMEM((nf, 8, 2 * rows), jnp.float32),
            pltpu.VMEM((len(CROSSED), 8, 384), jnp.float32),
            pltpu.VMEM((2, nb, 1, 2 * rows), jnp.float32),
            pltpu.VMEM((nb, 1, 2 * rows), jnp.float32),
            dma((nb, nc)), dma((nb, nc)), dma((nf, nc)), dma((nf, nc)),
            dma((nb,)), dma((nb,)), dma((nf,)), dma((nf,)), dma((2, nb)), dma((2, nb)),
        ],
        compiler_params=pltpu.CompilerParams(
            collective_id=0, has_side_effects=True, vmem_limit_bytes=56 << 20),
        cost_estimate=pl.CostEstimate(
            flops=36 * 2 * rows * 2 * rows * width, bytes_accessed=rows * width * 2, transcendentals=rows),
    )(embeddings, cluster.reshape(1, rows), order_key)


def solution(mesh):
    placed = (P(("dp", "grid"), None), P(("dp", "grid"), None), P(("dp", "grid")))
    return jax.shard_map(
        shards, mesh=mesh, in_specs=placed, out_specs=P(("dp", "grid")), check_vma=False
    )
```

```python
import functools

import jax
import jax.numpy as jnp
from jax import lax
from jax.experimental import pallas as pl
from jax.experimental.pallas import tpu as pltpu
from jax.sharding import PartitionSpec as P

MESH = pl.DeviceIdType.MESH
NT = (((1,), (1,)), ((), ()))
epsilon = 1e-06
scale = 65536.0

OFFSETS = {
    "o": (0, 0, 0), "a": (0, 0, 3), "b": (0, 1, 0), "c": (0, 3, 0),
    "d": (0, 3, 1), "e": (0, 3, 2), "f": (1, 0, 0), "g": (1, 1, 0),
    "h": (2, 1, 0), "i": (3, 0, 2), "j": (3, 0, 3), "k": (3, 1, 3),
}
FULL = "oabcdfghj"
HALF = "eik"
CHUNKS = (64, 64, 64, 64, 64)
ONE_WAY = {"bc", "eb", "ec", "eh", "hb", "hc", "if", "oo"}
ROWS_OF = "oabcdefghijk"
COLUMNS_OF = "oabcdfghj"
PROGRAM = (
    ">of3", ">oc4", ">ob0", ">of2", ">oc0", ">of4", ">oa0", ">oc1", ">ob1", ">ob2", ">oa1", ">oa2", "=o0", "=o1",
    "=o2", "=o3", "=o4", "!o", "*oo", "?f3", "=f3", "?c4", ">cd4", ">oc2", "=c4", "?b0", ">ob3", ">bg0", "=b0",
    "?a0", ">aj0", ">oa3", "=a0", "?f2", "=f2", "?c0", ">cd0", ">oc3", "=c0", "?b1", ">bg1", ">fg3", "=b1", "?a1",
    ">aj1", ">oa4", "=a1", "?f4", "=f4", "?c1", ">cd1", "=c1", "?b2", ">bg2", ">fg4", "=b2", "?d4", ">de4", "=d4",
    "?a2", ">aj2", "=a2", "?j0", ">ji0", "=j0", "?g0", ">gf0", ">gh0", "=g0", "?c2", "=c2", "?b3", ">jk0", "=b3",
    "?d0", ">cd2", "=d0", "?a3", ">aj3", "=a3", "?j1", ">ji1", "=j1", "?g1", ">gf1", ">gh1", "=g1", "?c3", "=c3",
    "?d1", ">cd3", "=d1", "?g3", ">jk1", "=g3", "?a4", ">aj4", "=a4", "?j2", ">ji2", "=j2", "*co", "!c", "*aoc",
    "?g2", ">gh2", "=g2", "?f0", "=f0", "?e4", ">de1", "?g4", ">gb4", ">jk2", "=g4", "?i0", "?j3", ">ji3", "=j3",
    "!a", "*goac", "?h0", ">gh3", "=h0", "?f1", "=f1", "?d2", ">de2", "=d2", "?k0", ">jk3", "?i1", "?j4", ">ji4",
    "=j4", "*foa", "!f", "!g", "*jcfg", "?h1", ">gh4", "=h1", "?d3", ">de3", "=d3", "?k1", ">jk4", "?i2", "?b4",
    "=b4", "!j", "*dafgj", "<j", "?h2", "=h2", "?e1", ">de0", "?k2", "?i3", "!d", "*bacdf", "<a", "?h3", "=h3",
    "?e2", "?k3", "?i4", "!b", "*iobdfg", "<i", "<g", "?h4", "=h4", "?e3", "?k4", "*hbocd", "!h", "*khcdf", "<k",
    "<d", "<f", "?e0", "*ecbh", "<e", "<h", "<b", "<c",
)
BLOCKS = FULL + HALF
SLOT = {b: n for n, b in enumerate(BLOCKS)}
CROSSED = sorted(ONE_WAY - {"oo"})
COLUMNS = COLUMNS_OF + "".join(sorted({i for _, i in CROSSED} - set(COLUMNS_OF)))


def between(source, target):
    return tuple((q - p) % 4 for p, q in zip(OFFSETS[source], OFFSETS[target]))


def kernel(rows, width, x_hbm, cluster_ref, key_ref, out_ref, x_ref, x_sem, full, half, meta, col_c, col_g, acc_row, acc_col, acc_cross, ret, back,
           send, recv, d2d_send, d2d_recv, m_send, m_recv, md_send, md_recv, r_send, r_recv):
    x, grid = lax.axis_index("dp"), lax.axis_index("grid")
    y, z, core = grid // 8, (grid // 2) % 4, grid % 2
    pair_rows = 2 * rows
    starts = [sum(CHUNKS[:n]) for n in range(len(CHUNKS))]
    mine = pl.multiple_of(core * rows, 16)

    def device(offset, which):
        dx, dy, dz = offset
        return ((x + dx) % 4, ((y + dy) % 4) * 8 + ((z + dz) % 4) * 2 + which)

    sibling = device((0, 0, 0), 1 - core)
    load = pltpu.make_async_copy(x_hbm, x_ref, x_sem)
    load.start()
    barrier = pltpu.get_barrier_semaphore()
    partners = {((0, 0, 0), 1)}
    for token in PROGRAM:
        if token[0] == ">":
            offset = between(token[1], token[2])
            partners |= {(offset, 0), (tuple(-v % 4 for v in offset), 0)}
    for b in BLOCKS[1:]:
        for offset in (OFFSETS[b], tuple(-v % 4 for v in OFFSETS[b])):
            partners.add((offset, 0))
            if b in COLUMNS:
                partners.add((offset, 1))
    partners = [device(offset, 1 - core if other else core) for offset, other in sorted(partners)]
    for n in partners:
        pl.semaphore_signal(barrier, inc=1, device_id=n, device_id_type=MESH)

    pending = []

    def copy(src, dst, send_sem, recv_sem, to):
        c = pltpu.make_async_remote_copy(
            src_ref=src, dst_ref=dst, send_sem=send_sem, recv_sem=recv_sem, device_id=to, device_id_type=MESH)
        c.start()
        pending.append(c)

    def arrived(here, sem):
        pltpu.make_async_copy(here, here, sem).wait()

    def place(b, s, which):
        if b in FULL:
            return full.at[SLOT[b], pl.ds(pl.multiple_of(which * rows + starts[s], 16), CHUNKS[s])]
        return half.at[SLOT[b] - len(FULL), pl.ds(starts[s], CHUNKS[s])]

    def hop(source, target, s):
        a, b, to = SLOT[source], SLOT[target], device(between(source, target), core)
        if s == 0:
            copy(meta.at[a, core], meta.at[b, core], m_send.at[b], m_recv.at[b], to)
        copy(place(source, s, core), place(target, s, core), send.at[b, s], recv.at[b, s], to)

    def got(b, s):
        n = SLOT[b]
        if s == 0:
            arrived(meta.at[n, core], m_recv.at[n])
        arrived(place(b, s, core), recv.at[n, s])

    def share(b, s):
        n = SLOT[b]
        if s == 0:
            copy(meta.at[n, core], meta.at[n, core], md_send.at[n], md_recv.at[n], sibling)
        copy(place(b, s, core), place(b, s, core), d2d_send.at[n, s], d2d_recv.at[n, s], sibling)

    def shared(b):
        n = SLOT[b]
        arrived(meta.at[n, 1 - core], md_recv.at[n])
        for s in range(len(CHUNKS)):
            arrived(place(b, s, 1 - core), d2d_recv.at[n, s])

    def columns(b):
        r = meta[SLOT[b], core]
        r = r[:, 0:384] + r[:, 320:704]
        t = jnp.transpose(jnp.broadcast_to(r, (128, 384)))[:rows]
        col_g[SLOT[b]] = t
        col_c[SLOT[b]] = jnp.floor(t * (1.0 / scale))

    low = lax.broadcasted_iota(jnp.int32, (1, 384), 1) < rows

    def turn(j, i):
        d = between(j, i)
        return (x if d[0] == 2 else y if d[1] == 2 else z) // 2

    def tiles(j, others):
        left = full[SLOT[j], pl.ds(mine, rows), :] if j in FULL else half[SLOT[j] - len(FULL)]
        cj, gj = col_c[SLOT[j]], col_g[SLOT[j]]
        best = acc_row[SLOT[j]]
        keys = {i: meta[SLOT[i], 0] + meta[SLOT[i], 1] for i in others}
        groups = {i: jnp.floor(keys[i] * (1.0 / scale)) for i in others}
        cross = {i: j + i in ONE_WAY and i != j for i in others}
        side = {i: lax.rem(core + turn(j, i), 2) for i in others if cross[i]}
        for i in side:
            r = meta[SLOT[i], side[i]]
            keys[i] = jnp.where(low, r[:, 0:384] + r[:, 320:704], -scale)
            groups[i] = jnp.floor(keys[i] * (1.0 / scale))
        units = [(i, n) for i in others for n in ((0, 128, rows - 128) if cross[i] else range(0, pair_rows, 128))]
        for first in range(0, len(units), 2):
            some = units[first:first + 2]
            right = [
                full[SLOT[i], pl.ds(pl.multiple_of(side[i] * rows + n, 16), 128), :] if cross[i]
                else full[SLOT[i], n:n + 128, :] for i, n in some]
            right = right[0] if len(some) == 1 else jnp.concatenate(right, axis=0)
            sims = lax.dot_general(left, right, NT, preferred_element_type=jnp.float32)
            for at, (i, n) in enumerate(some):
                t = jnp.where(cj == groups[i][:, n:n + 128], sims[:, at * 128:at * 128 + 128], -1.0)
                earlier = keys[i][:, n:n + 128] < gj
                best = jnp.maximum(best, jnp.where(earlier, t, -1.0))
                if i != j:
                    u = jnp.max(jnp.where(earlier, -1.0, t).reshape(rows // 8, 8, 128), axis=0)
                    if cross[i]:
                        at_ = {0: 0, 128: 128, rows - 128: 256}[n]
                        acc_cross[CROSSED.index(j + i), :, at_:at_ + 128] = u
                    else:
                        acc_col[SLOT[i], :, n:n + 128] = jnp.maximum(acc_col[SLOT[i], :, n:n + 128], u)
        acc_row[SLOT[j]] = best

    lanes = lax.broadcasted_iota(jnp.int32, (1, pair_rows), 1)
    ours = (lanes >= core * rows) & (lanes < (core + 1) * rows)

    def summary(b):
        m = jnp.full((1, pair_rows), -1.0, jnp.float32)
        if b in ROWS_OF:
            a = jnp.concatenate([acc_row[SLOT[b]], jnp.full((384 - rows, 128), -1.0, jnp.float32)], axis=0)
            r = jnp.max(jnp.transpose(a), axis=0, keepdims=True)[:, :rows]
            m = jnp.where(ours, jnp.concatenate([r, r], axis=1), m)
        if b in COLUMNS_OF:
            m = jnp.maximum(m, jnp.max(acc_col[SLOT[b]], axis=0, keepdims=True))
        for n, (j, i) in enumerate(CROSSED):
            if i == b:
                r = jnp.max(acc_cross[n], axis=0, keepdims=True)
                r = jnp.concatenate([
                    r[:, :rows - 128], jnp.maximum(r[:, rows - 128:256], r[:, 256:512 - (rows - 128)]),
                    r[:, 256 + 256 - (rows - 128):384]], axis=1)
                side = lax.rem(core + turn(j, i), 2)
                there = (lanes >= side * rows) & (lanes < (side + 1) * rows)
                m = jnp.where(there, jnp.maximum(m, jnp.concatenate([r, r], axis=1)), m)
        return m

    def owners(b):
        return (1,) if b == "o" else (0, 1) if b in COLUMNS else (0,)

    def give(b):
        n = SLOT[b]
        back[n] = summary(b)
        home = tuple(-v for v in OFFSETS[b])
        for which in owners(b):
            copy(back.at[n], ret.at[which, n], r_send.at[which, n], r_recv.at[which, n],
                 device(home, 1 - core if which else core))

    load.wait()
    values = x_ref[...].astype(jnp.float32)
    units = values * lax.rsqrt(jnp.sum(values * values, axis=1, keepdims=True) + epsilon)
    full[0, pl.ds(mine, rows), :] = units.astype(jnp.bfloat16)
    wide = lax.broadcasted_iota(jnp.int32, (1, 768), 1)
    own = (cluster_ref[...] * 65536 + key_ref[...].reshape(1, rows)).astype(jnp.float32)
    own = jnp.concatenate([own, own, jnp.zeros((1, 768 - 2 * rows), jnp.float32)], axis=1)
    meta[0, core] = jnp.where((wide >= core * rows) & (wide < (core + 1) * rows), own, 0.0)
    pl.semaphore_wait(barrier, len(partners))

    known = set()
    for token in PROGRAM:
        what, b = token[0], token[1]
        if what == ">":
            hop(b, token[2], int(token[3]))
        elif what == "?":
            got(b, int(token[2]))
        elif what == "=":
            share(b, int(token[2]))
        elif what == "!":
            if b == "o":
                acc_row[...] = jnp.full_like(acc_row, -1.0)
                acc_col[...] = jnp.full_like(acc_col, -1.0)
            shared(b)
        elif what == "*":
            if b not in known:
                columns(b)
                known.add(b)
            tiles(b, token[2:])
        else:
            give(b)
    if "o" in COLUMNS:
        give("o")
    total = back[0]
    for c in pending:
        c.wait_send()
    for b in BLOCKS:
        for which in owners(b):
            arrived(ret.at[which, SLOT[b]], r_recv.at[which, SLOT[b]])
            total = jnp.maximum(total, ret[which, SLOT[b]])
    out_ref[...] = jnp.where(core == 0, total[:, :rows], total[:, rows:]).reshape(rows)


def shards(embeddings, cluster, order_key):
    rows, width = embeddings.shape
    nf, nh, nb, nc = len(FULL), len(HALF), len(BLOCKS), len(CHUNKS)
    dma = pltpu.SemaphoreType.DMA
    return pl.pallas_call(
        functools.partial(kernel, rows, width),
        out_shape=jax.ShapeDtypeStruct((rows,), jnp.float32),
        in_specs=[pl.BlockSpec(memory_space=pl.ANY)] + [pl.BlockSpec(memory_space=pltpu.VMEM)] * 2,
        out_specs=pl.BlockSpec(memory_space=pltpu.VMEM),
        scratch_shapes=[
            pltpu.VMEM((rows, width), jnp.bfloat16),
            pltpu.SemaphoreType.DMA,
            pltpu.VMEM((nf, 2 * rows, width), jnp.bfloat16),
            pltpu.VMEM((nh, rows, width), jnp.bfloat16),
            pltpu.VMEM((nb, 2, 1, 768), jnp.float32),
            pltpu.VMEM((nb, rows, 128), jnp.float32),
            pltpu.VMEM((nb, rows, 128), jnp.float32),
            pltpu.VMEM((nb, rows, 128), jnp.float32),
            pltpu.VMEM((nf, 8, 2 * rows), jnp.float32),
            pltpu.VMEM((len(CROSSED), 8, 384), jnp.float32),
            pltpu.VMEM((2, nb, 1, 2 * rows), jnp.float32),
            pltpu.VMEM((nb, 1, 2 * rows), jnp.float32),
            dma((nb, nc)), dma((nb, nc)), dma((nf, nc)), dma((nf, nc)),
            dma((nb,)), dma((nb,)), dma((nf,)), dma((nf,)), dma((2, nb)), dma((2, nb)),
        ],
        compiler_params=pltpu.CompilerParams(
            collective_id=0, has_side_effects=True, vmem_limit_bytes=56 << 20),
        cost_estimate=pl.CostEstimate(
            flops=36 * 2 * rows * 2 * rows * width, bytes_accessed=rows * width * 2, transcendentals=rows),
    )(embeddings, cluster.reshape(1, rows), order_key)


def solution(mesh):
    placed = (P(("dp", "grid"), None), P(("dp", "grid"), None), P(("dp", "grid")))
    return jax.shard_map(
        shards, mesh=mesh, in_specs=placed, out_specs=P(("dp", "grid")), check_vma=False
    )
```

```python
import functools

import jax
import jax.numpy as jnp
from jax import lax
from jax.experimental import pallas as pl
from jax.experimental.pallas import tpu as pltpu
from jax.sharding import PartitionSpec as P

MESH = pl.DeviceIdType.MESH
NT = (((1,), (1,)), ((), ()))
epsilon = 1e-06
scale = 65536.0

OFFSETS = {
    "o": (0, 0, 0), "a": (0, 0, 3), "b": (0, 1, 0), "c": (0, 3, 0),
    "d": (0, 3, 1), "e": (0, 3, 2), "f": (1, 0, 0), "g": (1, 1, 0),
    "h": (2, 1, 0), "i": (3, 0, 2), "j": (3, 0, 3), "k": (3, 1, 3),
}
FULL = "oabcdfghj"
HALF = "eik"
CHUNKS = (64, 64, 64, 64, 64)
ONE_WAY = {"bc", "eb", "ec", "eh", "hb", "hc", "if", "oo"}
ROWS_OF = "oabcdefghijk"
COLUMNS_OF = "oabcdfghj"
PROGRAM = (
    ">of3", ">oc4", ">ob0", ">of2", ">oc0", ">of4", ">oa0", ">oc1", ">ob1", ">ob2", ">oa1", ">oa2", "=o0", "=o1",
    "=o2", "=o3", "=o4", "!o", "*oo", "?f3", "=f3", "?c4", ">cd4", ">oc2", "=c4", "?b0", ">ob3", ">bg0", "=b0",
    "?a0", ">aj0", ">oa3", "=a0", "?f2", "=f2", "?c0", ">cd0", ">oc3", "=c0", "?b1", ">bg1", ">fg3", "=b1", "?a1",
    ">aj1", ">oa4", "=a1", "?f4", "=f4", "?c1", ">cd1", "=c1", "?b2", ">bg2", ">fg4", "=b2", "?d4", ">de4", "=d4",
    "?a2", ">aj2", "=a2", "?j0", ">ji0", "=j0", "?g0", ">gf0", ">gh0", "=g0", "?c2", "=c2", "?b3", ">jk0", "=b3",
    "?d0", ">cd2", "=d0", "?a3", ">aj3", "=a3", "?j1", ">ji1", "=j1", "?g1", ">gf1", ">gh1", "=g1", "?c3", "=c3",
    "?d1", ">cd3", "=d1", "?g3", ">jk1", "=g3", "?a4", ">aj4", "=a4", "?j2", ">ji2", "=j2", "*co", "!c", "*aoc",
    "?g2", ">gh2", "=g2", "?f0", "=f0", "?e4", ">de1", "?g4", ">gb4", ">jk2", "=g4", "?i0", "?j3", ">ji3", "=j3",
    "!a", "*goac", "?h0", ">gh3", "=h0", "?f1", "=f1", "?d2", ">de2", "=d2", "?k0", ">jk3", "?i1", "?j4", ">ji4",
    "=j4", "*foa", "!f", "!g", "*jcfg", "?h1", ">gh4", "=h1", "?d3", ">de3", "=d3", "?k1", ">jk4", "?i2", "?b4",
    "=b4", "!j", "*dafgj", "<j", "?h2", "=h2", "?e1", ">de0", "?k2", "?i3", "!d", "*bacdf", "<a", "?h3", "=h3",
    "?e2", "?k3", "?i4", "!b", "*iobdfg", "<i", "<g", "?h4", "=h4", "?e3", "?k4", "*hbocd", "!h", "*khcdf", "<k",
    "<d", "<f", "?e0", "*ecbh", "<e", "<h", "<b", "<c",
)
BLOCKS = FULL + HALF
SLOT = {b: n for n, b in enumerate(BLOCKS)}
CROSSED = sorted(ONE_WAY - {"oo"})
COLUMNS = COLUMNS_OF + "".join(sorted({i for _, i in CROSSED} - set(COLUMNS_OF)))


def between(source, target):
    return tuple((q - p) % 4 for p, q in zip(OFFSETS[source], OFFSETS[target]))


def kernel(rows, width, x_hbm, cluster_ref, key_ref, out_ref, x_ref, x_sem, full, half, meta, col_c, col_g, acc_row, acc_col, acc_cross, ret, back,
           send, recv, d2d_send, d2d_recv, m_send, m_recv, md_send, md_recv, r_send, r_recv):
    x, grid = lax.axis_index("dp"), lax.axis_index("grid")
    y, z, core = grid // 8, (grid // 2) % 4, grid % 2
    pair_rows = 2 * rows
    starts = [sum(CHUNKS[:n]) for n in range(len(CHUNKS))]
    mine = pl.multiple_of(core * rows, 16)

    def device(offset, which):
        dx, dy, dz = offset
        return ((x + dx) % 4, ((y + dy) % 4) * 8 + ((z + dz) % 4) * 2 + which)

    sibling = device((0, 0, 0), 1 - core)
    load = pltpu.make_async_copy(x_hbm, x_ref, x_sem)
    load.start()
    barrier = pltpu.get_barrier_semaphore()
    partners = {((0, 0, 0), 1)}
    for token in PROGRAM:
        if token[0] == ">":
            offset = between(token[1], token[2])
            partners |= {(offset, 0), (tuple(-v % 4 for v in offset), 0)}
    for b in BLOCKS[1:]:
        for offset in (OFFSETS[b], tuple(-v % 4 for v in OFFSETS[b])):
            partners.add((offset, 0))
            if b in COLUMNS:
                partners.add((offset, 1))
    partners = [device(offset, 1 - core if other else core) for offset, other in sorted(partners)]
    for n in partners:
        pl.semaphore_signal(barrier, inc=1, device_id=n, device_id_type=MESH)

    pending = []

    def copy(src, dst, send_sem, recv_sem, to):
        c = pltpu.make_async_remote_copy(
            src_ref=src, dst_ref=dst, send_sem=send_sem, recv_sem=recv_sem, device_id=to, device_id_type=MESH)
        c.start()
        pending.append(c)

    def arrived(here, sem):
        pltpu.make_async_copy(here, here, sem).wait()

    def place(b, s, which):
        if b in FULL:
            return full.at[SLOT[b], pl.ds(pl.multiple_of(which * rows + starts[s], 16), CHUNKS[s])]
        return half.at[SLOT[b] - len(FULL), pl.ds(starts[s], CHUNKS[s])]

    def hop(source, target, s):
        a, b, to = SLOT[source], SLOT[target], device(between(source, target), core)
        if s == 0:
            copy(meta.at[a, core], meta.at[b, core], m_send.at[b], m_recv.at[b], to)
        copy(place(source, s, core), place(target, s, core), send.at[b, s], recv.at[b, s], to)

    def got(b, s):
        n = SLOT[b]
        if s == 0:
            arrived(meta.at[n, core], m_recv.at[n])
        arrived(place(b, s, core), recv.at[n, s])

    def share(b, s):
        n = SLOT[b]
        if s == 0:
            copy(meta.at[n, core], meta.at[n, core], md_send.at[n], md_recv.at[n], sibling)
        copy(place(b, s, core), place(b, s, core), d2d_send.at[n, s], d2d_recv.at[n, s], sibling)

    def shared(b):
        n = SLOT[b]
        arrived(meta.at[n, 1 - core], md_recv.at[n])
        for s in range(len(CHUNKS)):
            arrived(place(b, s, 1 - core), d2d_recv.at[n, s])

    def columns(b):
        r = meta[SLOT[b], core]
        r = r[:, 0:384] + r[:, 320:704]
        t = jnp.transpose(jnp.broadcast_to(r, (128, 384)))[:rows]
        col_g[SLOT[b]] = t
        col_c[SLOT[b]] = jnp.floor(t * (1.0 / scale))

    low = lax.broadcasted_iota(jnp.int32, (1, 384), 1) < rows

    def turn(j, i):
        d = between(j, i)
        return (x if d[0] == 2 else y if d[1] == 2 else z) // 2

    def tiles(j, others):
        left = full[SLOT[j], pl.ds(mine, rows), :] if j in FULL else half[SLOT[j] - len(FULL)]
        cj, gj = col_c[SLOT[j]], col_g[SLOT[j]]
        best = jnp.full((rows, 128), -1.0, jnp.float32)
        keys = {i: meta[SLOT[i], 0] + meta[SLOT[i], 1] for i in others}
        groups = {i: jnp.floor(keys[i] * (1.0 / scale)) for i in others}
        cross = {i: j + i in ONE_WAY and i != j for i in others}
        side = {i: lax.rem(core + turn(j, i), 2) for i in others if cross[i]}
        for i in side:
            r = meta[SLOT[i], side[i]]
            keys[i] = jnp.where(low, r[:, 0:384] + r[:, 320:704], -scale)
            groups[i] = jnp.floor(keys[i] * (1.0 / scale))
        units = [(i, n) for i in others for n in ((0, 128, rows - 128) if cross[i] else range(0, pair_rows, 128))]
        for first in range(0, len(units), 2):
            some = units[first:first + 2]
            right = [
                full[SLOT[i], pl.ds(pl.multiple_of(side[i] * rows + n, 16), 128), :] if cross[i]
                else full[SLOT[i], n:n + 128, :] for i, n in some]
            right = right[0] if len(some) == 1 else jnp.concatenate(right, axis=0)
            sims = lax.dot_general(left, right, NT, preferred_element_type=jnp.float32)
            for at, (i, n) in enumerate(some):
                t = jnp.where(cj == groups[i][:, n:n + 128], sims[:, at * 128:at * 128 + 128], -1.0)
                earlier = keys[i][:, n:n + 128] < gj
                best = jnp.maximum(best, jnp.where(earlier, t, -1.0))
                if i != j:
                    u = jnp.max(jnp.where(earlier, -1.0, t).reshape(rows // 8, 8, 128), axis=0)
                    if cross[i]:
                        at_ = {0: 0, 128: 128, rows - 128: 256}[n]
                        acc_cross[CROSSED.index(j + i), :, at_:at_ + 128] = u
                    else:
                        acc_col[SLOT[i], :, n:n + 128] = jnp.maximum(acc_col[SLOT[i], :, n:n + 128], u)
        acc_row[SLOT[j]] = best

    lanes = lax.broadcasted_iota(jnp.int32, (1, pair_rows), 1)
    ours = (lanes >= core * rows) & (lanes < (core + 1) * rows)

    def summary(b):
        m = jnp.full((1, pair_rows), -1.0, jnp.float32)
        if b in ROWS_OF:
            a = jnp.concatenate([acc_row[SLOT[b]], jnp.full((384 - rows, 128), -1.0, jnp.float32)], axis=0)
            r = jnp.max(jnp.transpose(a), axis=0, keepdims=True)[:, :rows]
            m = jnp.where(ours, jnp.concatenate([r, r], axis=1), m)
        if b in COLUMNS_OF:
            m = jnp.maximum(m, jnp.max(acc_col[SLOT[b]], axis=0, keepdims=True))
        for n, (j, i) in enumerate(CROSSED):
            if i == b:
                r = jnp.max(acc_cross[n], axis=0, keepdims=True)
                r = jnp.concatenate([
                    r[:, :rows - 128], jnp.maximum(r[:, rows - 128:256], r[:, 256:512 - (rows - 128)]),
                    r[:, 256 + 256 - (rows - 128):384]], axis=1)
                side = lax.rem(core + turn(j, i), 2)
                there = (lanes >= side * rows) & (lanes < (side + 1) * rows)
                m = jnp.where(there, jnp.maximum(m, jnp.concatenate([r, r], axis=1)), m)
        return m

    def owners(b):
        return (1,) if b == "o" else (0, 1) if b in COLUMNS else (0,)

    def give(b):
        n = SLOT[b]
        back[n] = summary(b)
        home = tuple(-v for v in OFFSETS[b])
        for which in owners(b):
            copy(back.at[n], ret.at[which, n], r_send.at[which, n], r_recv.at[which, n],
                 device(home, 1 - core if which else core))

    load.wait()
    values = x_ref[...].astype(jnp.float32)
    units = values * lax.rsqrt(jnp.sum(values * values, axis=1, keepdims=True) + epsilon)
    full[0, pl.ds(mine, rows), :] = units.astype(jnp.bfloat16)
    wide = lax.broadcasted_iota(jnp.int32, (1, 768), 1)
    own = (cluster_ref[...] * 65536 + key_ref[...].reshape(1, rows)).astype(jnp.float32)
    own = jnp.concatenate([own, own, jnp.zeros((1, 768 - 2 * rows), jnp.float32)], axis=1)
    meta[0, core] = jnp.where((wide >= core * rows) & (wide < (core + 1) * rows), own, 0.0)
    pl.semaphore_wait(barrier, len(partners))

    known = set()
    for token in PROGRAM:
        what, b = token[0], token[1]
        if what == ">":
            hop(b, token[2], int(token[3]))
        elif what == "?":
            got(b, int(token[2]))
        elif what == "=":
            share(b, int(token[2]))
        elif what == "!":
            if b == "o":
                acc_col[...] = jnp.full_like(acc_col, -1.0)
            shared(b)
        elif what == "*":
            if b not in known:
                columns(b)
                known.add(b)
            tiles(b, token[2:])
        else:
            give(b)
    if "o" in COLUMNS:
        give("o")
    total = back[0]
    for c in pending:
        c.wait_send()
    for b in BLOCKS:
        for which in owners(b):
            arrived(ret.at[which, SLOT[b]], r_recv.at[which, SLOT[b]])
            total = jnp.maximum(total, ret[which, SLOT[b]])
    out_ref[...] = jnp.where(core == 0, total[:, :rows], total[:, rows:]).reshape(rows)


def shards(embeddings, cluster, order_key):
    rows, width = embeddings.shape
    nf, nh, nb, nc = len(FULL), len(HALF), len(BLOCKS), len(CHUNKS)
    dma = pltpu.SemaphoreType.DMA
    return pl.pallas_call(
        functools.partial(kernel, rows, width),
        out_shape=jax.ShapeDtypeStruct((rows,), jnp.float32),
        in_specs=[pl.BlockSpec(memory_space=pl.ANY)] + [pl.BlockSpec(memory_space=pltpu.VMEM)] * 2,
        out_specs=pl.BlockSpec(memory_space=pltpu.VMEM),
        scratch_shapes=[
            pltpu.VMEM((rows, width), jnp.bfloat16),
            pltpu.SemaphoreType.DMA,
            pltpu.VMEM((nf, 2 * rows, width), jnp.bfloat16),
            pltpu.VMEM((nh, rows, width), jnp.bfloat16),
            pltpu.VMEM((nb, 2, 1, 768), jnp.float32),
            pltpu.VMEM((nb, rows, 128), jnp.float32),
            pltpu.VMEM((nb, rows, 128), jnp.float32),
            pltpu.VMEM((nb, rows, 128), jnp.float32),
            pltpu.VMEM((nf, 8, 2 * rows), jnp.float32),
            pltpu.VMEM((len(CROSSED), 8, 384), jnp.float32),
            pltpu.VMEM((2, nb, 1, 2 * rows), jnp.float32),
            pltpu.VMEM((nb, 1, 2 * rows), jnp.float32),
            dma((nb, nc)), dma((nb, nc)), dma((nf, nc)), dma((nf, nc)),
            dma((nb,)), dma((nb,)), dma((nf,)), dma((nf,)), dma((2, nb)), dma((2, nb)),
        ],
        compiler_params=pltpu.CompilerParams(
            collective_id=0, has_side_effects=True, vmem_limit_bytes=56 << 20),
        cost_estimate=pl.CostEstimate(
            flops=36 * 2 * rows * 2 * rows * width, bytes_accessed=rows * width * 2, transcendentals=rows),
    )(embeddings, cluster.reshape(1, rows), order_key)


def solution(mesh):
    placed = (P(("dp", "grid"), None), P(("dp", "grid"), None), P(("dp", "grid")))
    return jax.shard_map(
        shards, mesh=mesh, in_specs=placed, out_specs=P(("dp", "grid")), check_vma=False
    )
```
